32 devices in a mesh: runs: 2 (over x), area: 16 (over z, y, core).
Axes of the slice: x: 2, y: 2, z: 4, core: 2. Of those that a mesh axis runs over, the one named last changes fastest.
Arguments:
- history: bfloat16 [4, 32, 16384], P(None, 'runs', 'area'), parts along dimension 1, may hold values from 0 to 1
- drive: bfloat16 [32, 16384], P('runs', 'area'), parts along dimension 0, may hold values from -6 to 6
- leak: float32 [32768], P(('runs', 'area')), parts along dimension 0, may hold values from 0.1 to 0.9
- inhibition: float32 [16], P('runs'), parts along dimension 0, may hold values from 0.5 to 4
- section: int32 [16], replicated, may hold values from 0 to 7, never falling along the last dimension, each value on 1 to 6 neighbouring positions
- link_source: int32 [768, 1], P('area'), may hold values from 0 to 15; in each aligned block of 48 rows (0 to 47, 48 to 95, ...) at most 3 rows name the same one
- link_block: int32 [768], P('area'), may hold values from 0 to 3
- link_target: int32 [768], P('area'), may hold values from 0 to 3
- link_delay: int32 [768], P('area'), may hold values from 2 to 4
- remote_weight: bfloat16 [1536, 256, 256], P(('runs', 'area')), parts along dimension 0, may hold values from -0.375 to 0.375
- local_block: int32 [256], P('area'), may hold values from 0 to 3
- local_target: int32 [256], P('area'), may hold values from 0 to 3
- local_delay: int32 [256], P('area'), may hold values from 1 to 4
- local_weight: bfloat16 [512, 256, 256], P(('runs', 'area')), parts along dimension 0, may hold values from -0.375 to 0.375
Outputs:
- rates: bfloat16 [32, 16384], P('runs', 'area'), parts along dimension 0
The draws below stay inside these ranges and needn't reach their ends.
There are 2 independent parts, one for each index of `runs`. The reference program is written for one: setup_inputs(seed, part) draws one part's arguments, and reference() takes and returns one part's arrays. A program takes and returns all parts, laid end to end along the dimension named above; an argument that names none is the same for every part. Nothing has to cross between parts.
Inputs may be any that keep to these rules, and one draw needn't show every extreme that they name: `section`: Nondecreasing; every area covers 1 to 6 consecutive indices, and some area covers exactly 6. `link_source`: among the 48 remote tiles of one index of area, no index of area is named more than 3 times, a bound that some block reaches.
All inputs are finite; a program needn't handle non-finite values.
Results may differ from the reference program's by a relative error of at most 0.005.
Values may be sent and summed in bfloat16 or wider, within the bound.
A program may use at most 128 MiB of HBM per device.

```python
import math
import jax
import jax.numpy as jnp
import numpy as np

POP = 256
BLK_DEV = 4
TRIALS = 16
LINKS = 48
LOCAL = 16
DMAX = 4
DMIN = 2
STEPS = 6
MOST_SEC = 6
AREAS = 8
CAP = 3
NEURONS = 16384
N_AREA = 16


def plant(drawn, rng, low, high):
    dims = drawn.shape
    spot = [jax.random.randint(jax.random.fold_in(rng, axis), (), 0, dims[axis]) for axis in range(len(dims))]
    drawn = drawn.at[tuple(spot)].set(low)
    longest = dims.index(max(dims))
    spot[longest] = (spot[longest] + 1) % dims[longest]
    return drawn.at[tuple(spot)].set(high)


def block_scale(rng, shape, split, smallest, largest):
    factor_of = 1.0
    for dim, blocks in split:
        heights = jax.random.uniform(jax.random.fold_in(jax.random.fold_in(rng, 6), dim), (blocks,), jnp.float32, smallest / len(split), largest / len(split))
        factor_of = factor_of * jnp.repeat(jnp.exp(heights), shape[dim] // blocks).reshape((-1,) + (1,) * (len(shape) - 1 - dim))
    return factor_of


def split_up(number_of, total, limit, lean):
    portions = [(1 << 20) // math.isqrt(standing ** lean) + 1 for standing in range(2, number_of + 1)]
    surplus, holding = total - limit - (number_of - 1), [1] * (number_of - 1)
    while surplus > 0:
        free = [i for i in range(number_of - 1) if holding[i] < limit]
        whole, left = sum([portions[i] for i in free]), surplus
        for i in free:
            extra = min(limit - holding[i], max(1, left * portions[i] // whole), surplus)
            holding[i] = holding[i] + extra
            surplus = surplus - extra
    return np.array([limit] + holding)


def ragged_sizes(key, count, total, bound, slope):
    if count == 2:
        one = jax.random.randint(key, (), max(1, total - bound), min(bound, total - 1) + 1)
        return jnp.stack([one, total - one])
    tallies = jnp.asarray(split_up(count, total, bound, slope), jnp.int32)
    twos = (count - 1) // 2
    giver, receiver = tallies[1:1 + 2 * twos:2], tallies[2:2 + 2 * twos:2]
    margin = jnp.minimum(giver - 1, bound - receiver)
    passed = jax.random.randint(jax.random.fold_in(key, 1), (twos,), 0, 1 << 20) % (margin + 1)
    tallies = tallies.at[1:1 + 2 * twos:2].set(giver - passed).at[2:2 + 2 * twos:2].set(receiver + passed)
    return tallies[jax.random.permutation(jax.random.fold_in(key, 2), count)]


def shared_out(own_key, own, number, rows, count, top, most, skew):
    order = jax.random.permutation(own_key, count)
    crowded, ordinary = load_shares(count, rows * top, most, skew, True), load_shares(count, rows * top, most, skew, False)
    places = jnp.arange(count)

    def named(sizes, offset_by):
        used = int((sizes > 0).sum())
        fixed = max(1, used // 4)
        shifted = fixed + (places - fixed + offset_by * (used - fixed)) % max(1, count - fixed)
        return jnp.zeros((count,), jnp.int32).at[order[jnp.where(places < fixed, places, shifted)]].set(jnp.asarray(sizes, jnp.int32))

    sizes = jnp.where(number % 4 == 0, named(crowded, number // 4), named(ordinary, number - number // 4 - 1))
    mixed = jax.random.permutation(jax.random.fold_in(own, 3), count)
    giver, receiver = mixed[0:count // 2 * 2:2], mixed[1:count // 2 * 2:2]
    room = jnp.minimum(sizes[giver] - 1, most - sizes[receiver]) // 2
    room = jnp.where((giver == order[0]) | (receiver == order[0]) | (sizes[receiver] == 0), 0, jnp.maximum(room, 0))
    shifted = jax.random.randint(jax.random.fold_in(own, 4), (count // 2,), 0, 1 << 20) % (room + 1)
    sizes = sizes.at[giver].add(-shifted).at[receiver].add(shifted)
    items = jnp.searchsorted(jnp.cumsum(sizes), jnp.arange(rows * top), side="right").astype(jnp.int32)
    listing = items.reshape(top, rows).T
    listing = listing[jax.random.permutation(jax.random.fold_in(own, 1), rows)]
    offset_by = jax.random.randint(jax.random.fold_in(own, 2), (rows, 1), 0, top)
    return jnp.take_along_axis(listing, (jnp.arange(top)[None, :] + offset_by) % top, axis=1)


def load_shares(amount, total, limit, skew, full):
    loads = [(1 << 20) // math.isqrt(grade ** skew) + 1 for grade in range(1, amount + 1)]
    largest = limit if full else min(limit, max(-(-total // amount), total * loads[0] // sum(loads)))
    least = 1 if total - largest >= amount - 1 else 0
    given, surplus = [largest] + [least] * (amount - 1), total - largest - least * (amount - 1)
    while surplus > 0:
        free = [i for i in range(1, amount) if given[i] < largest] or [i for i in range(1, amount) if given[i] < limit]
        pool, remaining = sum([loads[i] for i in free]), surplus
        for i in free:
            addition = min(limit - given[i], max(1, remaining * loads[i] // pool), surplus)
            given[i] = given[i] + addition
            surplus = surplus - addition
    return np.array(given)


def centred(key, extent, width, bound, cuts=(), held_as=jnp.bfloat16):
    values = jax.random.normal(key, extent, jnp.float32) * width
    if len(cuts) > 0:
        values = block_scale(key, extent, cuts, -0.22, 0.18) * values
    return jnp.clip(values, min=-bound, max=bound).astype(held_as)


def setup_inputs(seed: int = 0, part: int = 0) -> dict:
    streams_of = jax.random.split(jax.random.key(seed), 15)
    own_keys = jax.random.split(jax.random.fold_in(streams_of[14], part), 15)
    history = jnp.clip(1.0 * jax.random.uniform(own_keys[0], (DMAX, TRIALS, NEURONS), jnp.float32) ** block_scale(own_keys[0], (DMAX, TRIALS, NEURONS), ((2, 16),), -0.2, 0.2), 0.0, 1.0).astype(jnp.bfloat16)
    drive = centred(own_keys[1], (TRIALS, NEURONS), 1.0, 6.0, ((1, 16),))
    leak = jnp.clip(jnp.exp(math.log(0.9) - 2.1972245 * jax.random.uniform(own_keys[2], (NEURONS,), jnp.float32) ** block_scale(own_keys[2], (NEURONS,), ((0, 16),), -0.2, 0.2)), 0.1, 0.9)
    inhibition = jnp.clip(jnp.exp(jax.random.uniform(own_keys[3], (AREAS,), jnp.float32, math.log(0.5), math.log(4.0))), 0.5, 4.0)
    section = jnp.searchsorted(jnp.cumsum(ragged_sizes(streams_of[4], AREAS, N_AREA, MOST_SEC, 2)), jnp.arange(N_AREA), side="right").astype(jnp.int32)
    link_source_keys = jax.random.split(jax.random.fold_in(streams_of[5], 1), (N_AREA * LINKS) // LINKS)
    link_source_turns = jax.random.permutation(jax.random.fold_in(streams_of[5], 3), (N_AREA * LINKS) // LINKS)
    link_source = jax.vmap(lambda own, number: shared_out(jax.random.fold_in(streams_of[5], 2), own, number, LINKS, N_AREA, 1, CAP, 2))(link_source_keys, link_source_turns).reshape((N_AREA * LINKS, 1))
    link_block = plant(jax.random.randint(streams_of[6], (N_AREA * LINKS,), 0, BLK_DEV), jax.random.fold_in(streams_of[6], 1), 0, BLK_DEV - 1).astype(jnp.int32)
    link_target = plant(jax.random.randint(streams_of[7], (N_AREA * LINKS,), 0, BLK_DEV), jax.random.fold_in(streams_of[7], 1), 0, BLK_DEV - 1).astype(jnp.int32)
    link_delay = plant(jax.random.randint(streams_of[8], (N_AREA * LINKS,), DMIN, DMAX + 1), jax.random.fold_in(streams_of[8], 1), DMIN, DMAX).astype(jnp.int32)
    remote_weight = centred(own_keys[9], (N_AREA * LINKS, POP, POP), POP ** -0.5, 0.375, ((0, 16),))
    local_block = plant(jax.random.randint(streams_of[10], (N_AREA * LOCAL,), 0, BLK_DEV), jax.random.fold_in(streams_of[10], 1), 0, BLK_DEV - 1).astype(jnp.int32)
    local_target = plant(jax.random.randint(streams_of[11], (N_AREA * LOCAL,), 0, BLK_DEV), jax.random.fold_in(streams_of[11], 1), 0, BLK_DEV - 1).astype(jnp.int32)
    local_delay = plant(jax.random.randint(streams_of[12], (N_AREA * LOCAL,), 1, DMAX + 1), jax.random.fold_in(streams_of[12], 1), 1, DMAX).astype(jnp.int32)
    local_weight = centred(own_keys[13], (N_AREA * LOCAL, POP, POP), POP ** -0.5, 0.375, ((0, 16),))
    return dict(history=history, drive=drive, leak=leak, inhibition=inhibition, section=section, link_source=link_source, link_block=link_block, link_target=link_target, link_delay=link_delay, remote_weight=remote_weight, local_block=local_block, local_target=local_target, local_delay=local_delay, local_weight=local_weight)


def reference(history, drive, leak, inhibition, section, link_source, link_block, link_target, link_delay, remote_weight, local_block, local_target, local_delay, local_weight):
    block_total = N_AREA * BLK_DEV
    states = history.reshape(DMAX, TRIALS, block_total, POP).transpose(0, 2, 1, 3)
    link_owner = jnp.arange(N_AREA * LINKS, dtype=jnp.int32) // LINKS
    remote_source = link_source[:, 0] * BLK_DEV + link_block
    remote_target = link_owner * BLK_DEV + link_target
    local_owner = jnp.arange(N_AREA * LOCAL, dtype=jnp.int32) // LOCAL
    local_source = local_owner * BLK_DEV + local_block
    local_dest = local_owner * BLK_DEV + local_target
    drive_blocks = drive.astype(jnp.float32).reshape(TRIALS, block_total, POP).transpose(1, 0, 2)
    leak_blocks = leak.reshape(block_total, 1, POP)
    block_area = section[jnp.arange(block_total, dtype=jnp.int32) // BLK_DEV]
    area_count = jnp.sum((section[None, :] == jnp.arange(AREAS, dtype=jnp.int32)[:, None]).astype(jnp.float32), axis=1) * (BLK_DEV * POP)
    inhibit_blocks = inhibition[block_area][:, None, None]
    remote_float = remote_weight.astype(jnp.float32)
    local_float = local_weight.astype(jnp.float32)
    fresh = states[0]
    for step_index in range(STEPS):
        previous = states[0].astype(jnp.float32)
        block_sums = jnp.sum(previous, axis=2)
        totals = jax.ops.segment_sum(block_sums, block_area, AREAS)
        means = totals / area_count[:, None]
        mean_blocks = means[block_area][:, :, None]
        remote_in = states[link_delay - 1, remote_source].astype(jnp.float32)
        remote_terms = jnp.einsum("ltp,lpq->ltq", remote_in, remote_float)
        local_in = states[local_delay - 1, local_source].astype(jnp.float32)
        local_terms = jnp.einsum("ltp,lpq->ltq", local_in, local_float)
        current = jax.ops.segment_sum(remote_terms, remote_target, block_total) + jax.ops.segment_sum(local_terms, local_dest, block_total)
        driven = jax.nn.sigmoid(current + drive_blocks - inhibit_blocks * mean_blocks)
        fresh = ((1.0 - leak_blocks) * previous + leak_blocks * driven).astype(jnp.bfloat16)
        states = jnp.concatenate([fresh[None], states[:-1]], axis=0)
    return fresh.transpose(1, 0, 2).reshape(TRIALS, block_total * POP)
```

```python
import functools

import jax
import jax.numpy as jnp
from jax import lax
from jax.experimental import pallas as pl
from jax.experimental.pallas import tpu as pltpu
from jax.sharding import PartitionSpec as P

STEPS = 6
DMAX = 4
SLICES = STEPS - 2 + DMAX
UNROLL = 8
MESH = pl.DeviceIdType.MESH


def kernel(nz, ny, *refs):
    (
        history, drive, leak, inhibition, section, link_source, link_block, link_target, link_delay,
        remote_weight, local_block, local_target, local_delay, local_weight, out,
    ) = refs[:15]
    rest = refs[15:]
    gathered = rest[:SLICES]
    own = rest[SLICES : SLICES + DMAX + STEPS - 1]
    (
        w_remote, w_local, sums, area_mask, place,
        w_sem, sum_send, sum_recv, z_send, z_recv, y_send, y_recv, c_send, c_recv, d_send, d_recv,
    ) = rest[SLICES + DMAX + STEPS - 1 :]
    n = nz * ny * 2
    trials, width = drive.shape
    pop = w_remote.shape[1]
    blocks = width // pop
    links = link_block.shape[0]
    locals_ = local_block.shape[0]

    me = lax.axis_index("area")
    core = lax.rem(me, 2)
    y = lax.rem(me // 2, ny)
    z = me // (2 * ny)
    line = (y * 2 + core) * nz
    line_y = ((1 - y) * 2 + core) * nz
    my_place = line + z
    sibling = me + 1 - 2 * core
    across = me + (1 - 2 * y) * 2

    barrier = pltpu.get_barrier_semaphore()

    @pl.loop(1, n)
    def _(k):
        pl.semaphore_signal(barrier, inc=1, device_id={"area": lax.rem(me + k, n)}, device_id_type=MESH)

    load_local = pltpu.make_async_copy(local_weight, w_local, w_sem.at[0])
    load_remote = pltpu.make_async_copy(remote_weight, w_remote, w_sem.at[1])
    load_local.start()
    load_remote.start()

    def keep(s, values):
        for b in range(blocks):
            own[s][b] = values[b]
            if s < SLICES:
                gathered[s][my_place * blocks + b] = values[b]

    for s in range(DMAX):
        keep(s, [history[DMAX - 1 - s, :, b * pop : (b + 1) * pop] for b in range(blocks)])

    rows = lax.broadcasted_iota(jnp.int32, (trials, 128), 0)
    lanes = lax.broadcasted_iota(jnp.int32, (trials, 128), 1)
    diagonal = rows == lanes

    def put_sum(t, values):
        total = values[0].astype(jnp.float32)
        for b in range(1, blocks):
            total = total + values[b].astype(jnp.float32)
        column = jnp.sum(total, axis=1, keepdims=True)
        row = jnp.sum(jnp.where(diagonal, column, 0.0), axis=0, keepdims=True)
        sums[t, pl.ds(me, 1), :] = row

    def send_sums(t):
        @pl.loop(1, n)
        def _(k):
            pltpu.make_async_remote_copy(
                src_ref=sums.at[t, pl.ds(me, 1)],
                dst_ref=sums.at[t, pl.ds(me, 1)],
                send_sem=sum_send.at[t],
                recv_sem=sum_recv.at[t],
                device_id={"area": lax.rem(me + k, n)},
                device_id_type=MESH,
            ).start()

    def await_bytes(ref, sem):
        pltpu.make_async_copy(ref, ref, sem).wait()

    def part(s, start, count):
        return gathered[s].at[pl.ds(start * blocks, count * blocks)]

    def z_start(s):
        @pl.loop(1, nz)
        def _(k):
            there = lax.rem(z + k, nz)
            pltpu.make_async_remote_copy(
                src_ref=part(s, my_place, 1),
                dst_ref=part(s, my_place, 1),
                send_sem=z_send.at[s],
                recv_sem=z_recv.at[s],
                device_id={"area": (there * ny + y) * 2 + core},
                device_id_type=MESH,
            ).start()

    def relay(s, start, target, send, recv):
        return pltpu.make_async_remote_copy(
            src_ref=part(s, start, nz),
            dst_ref=part(s, start, nz),
            send_sem=send.at[s],
            recv_sem=recv.at[s],
            device_id={"area": target},
            device_id_type=MESH,
        )

    def z_done(s):
        await_bytes(part(s, line, nz - 1), z_recv.at[s])
        if ny == 2:
            relay(s, line, across, y_send, y_recv).start()
        relay(s, line, sibling, c_send, c_recv).start()

    def y_done(s):
        if ny == 2:
            await_bytes(part(s, line_y, nz), y_recv.at[s])
            relay(s, line_y, sibling, d_send, d_recv).start()

    def c_done(s):
        await_bytes(part(s, line, nz), c_recv.at[s])
        if ny == 2:
            await_bytes(part(s, line_y, nz), d_recv.at[s])

    put_sum(0, [own[DMAX - 1][b] for b in range(blocks)])
    pl.semaphore_wait(barrier, n - 1)
    send_sums(0)
    for s in range(DMAX):
        z_start(s)

    @pl.loop(0, links)
    def _(l):
        q = link_source[l]
        at = (lax.rem(q // 2, ny) * 2 + lax.rem(q, 2)) * nz + q // (2 * ny)
        place[l] = at * blocks + link_block[l]

    my_area = section[me]
    count = jnp.float32(0.0)
    for q in range(n):
        same = jnp.where(section[q] == my_area, 1.0, 0.0).astype(jnp.float32)
        count = count + same
        area_mask[q : q + 1, :] = jnp.full((1, 128), same, jnp.float32)
    inhibit = inhibition[my_area]
    neurons = jnp.full((1, 128), count * float(width), jnp.float32)

    zero = jnp.zeros((trials, pop), jnp.bfloat16)

    def dots(acc, total, sources, first, at_ref, delay_ref, target_ref, weight):
        def body(g, acc):
            columns = []
            for u in range(UNROLL):
                l = g * UNROLL + u
                at, delay, target = at_ref[l], delay_ref[l], target_ref[l]
                x = sources[-1][at]
                for i in range(len(sources) - 2, -1, -1):
                    x = lax.select(delay == first + i, sources[i][at], x)
                columns.append(jnp.concatenate([lax.select(target == b, x, zero) for b in range(blocks)], axis=0))
            lhs = jnp.concatenate(columns, axis=1)
            w = weight[pl.ds(g * UNROLL, UNROLL)].reshape(UNROLL * pop, pop)
            return acc + jnp.dot(lhs, w, preferred_element_type=jnp.float32)

        return lax.fori_loop(0, total // UNROLL, body, acc)

    def local_dots(t, acc):
        return dots(
            acc, locals_, [own[t + DMAX - d] for d in range(1, DMAX + 1)], 1, local_block, local_delay, local_target, w_local
        )

    def remote_dots(t, acc):
        return dots(
            acc, links, [gathered[t + DMAX - d] for d in range(2, DMAX + 1)], 2, place, link_delay, link_target, w_remote
        )

    def finish(t, acc):
        await_bytes(sums.at[t, pl.ds(0, n - 1)], sum_recv.at[t])
        total = jnp.sum(sums[t] * area_mask[...], axis=0, keepdims=True)
        row = inhibit * (total / neurons)
        held = jnp.sum(jnp.where(diagonal, row, 0.0), axis=1, keepdims=True)
        fresh = []
        for b in range(blocks):
            cut = slice(b * pop, (b + 1) * pop)
            gain = leak[:, cut]
            pushed = acc[b * trials : (b + 1) * trials] + drive[:, cut].astype(jnp.float32) - held
            previous = own[t + DMAX - 1][b].astype(jnp.float32)
            fresh.append(((1.0 - gain) * previous + gain * jax.nn.sigmoid(pushed)).astype(jnp.bfloat16))
        return fresh

    for t in range(STEPS):
        acc = jnp.zeros((blocks * trials, pop), jnp.float32)
        if t == 0:
            load_local.wait()
            acc = local_dots(t, acc)
            z_done(0)
            z_done(1)
            y_done(0)
            z_done(2)
            y_done(1)
            z_done(3)
            y_done(2)
            load_remote.wait()
            for s in range(DMAX - 1):
                c_done(s)
            acc = remote_dots(t, acc)
            y_done(3)
        else:
            if t >= 2:
                y_done(t + DMAX - 2)
            acc = local_dots(t, acc)
            c_done(t + DMAX - 2)
            acc = remote_dots(t, acc)
            if t + DMAX - 1 < SLICES:
                z_done(t + DMAX - 1)
        fresh = finish(t, acc)
        if t == STEPS - 1:
            for b in range(blocks):
                out[:, b * pop : (b + 1) * pop] = fresh[b]
        else:
            keep(t + DMAX, fresh)
            put_sum(t + 1, fresh)
            send_sums(t + 1)
            if t + DMAX < SLICES:
                z_start(t + DMAX)

    for t in range(STEPS):
        await_bytes(sums.at[t, pl.ds(0, n - 1)], sum_send.at[t])
    for s in range(SLICES):
        await_bytes(part(s, line, nz - 1), z_send.at[s])
        await_bytes(part(s, line, nz), c_send.at[s])
        if ny == 2:
            await_bytes(part(s, line, nz), y_send.at[s])
            await_bytes(part(s, line_y, nz), d_send.at[s])


def local(nz, ny, *args):
    (history, drive, leak, inhibition, section, link_source, *others) = args
    remote_weight, local_weight = others[3], others[7]
    depth, trials, width = history.shape
    pop = remote_weight.shape[1]
    blocks = width // pop
    n = nz * ny * 2
    vmem, smem, hbm = (
        pl.BlockSpec(memory_space=pltpu.VMEM),
        pl.BlockSpec(memory_space=pltpu.SMEM),
        pl.BlockSpec(memory_space=pl.ANY),
    )
    dma = pltpu.SemaphoreType.DMA
    return pl.pallas_call(
        functools.partial(kernel, nz, ny),
        out_shape=jax.ShapeDtypeStruct((trials, width), jnp.bfloat16),
        in_specs=[vmem, vmem, vmem, smem, smem, smem, smem, smem, smem, hbm, smem, smem, smem, hbm],
        out_specs=vmem,
        scratch_shapes=[
            *[pltpu.VMEM((n * blocks, trials, pop), jnp.bfloat16) for _ in range(SLICES)],
            *[pltpu.VMEM((blocks, trials, pop), jnp.bfloat16) for _ in range(DMAX + STEPS - 1)],
            pltpu.VMEM(remote_weight.shape, jnp.bfloat16),
            pltpu.VMEM(local_weight.shape, jnp.bfloat16),
            pltpu.VMEM((STEPS, n, 128), jnp.float32),
            pltpu.VMEM((n, 128), jnp.float32),
            pltpu.SMEM((link_source.shape[0],), jnp.int32),
            dma((2,)),
            dma((STEPS,)),
            dma((STEPS,)),
            *[dma((SLICES,)) for _ in range(8)],
        ],
        compiler_params=pltpu.CompilerParams(
            collective_id=0, has_side_effects=True, vmem_limit_bytes=52 * 1024 * 1024
        ),
    )(history, drive, leak.reshape(1, -1), inhibition, section, link_source.reshape(-1), *others)


def solution(mesh):
    ny = 2 if mesh.shape["runs"] == 2 else 1
    nz = mesh.shape["area"] // (2 * ny)
    placed = (
        P(None, "runs", "area"),
        P("runs", "area"),
        P(("runs", "area")),
        P("runs"),
        P(),
        P("area", None),
        P("area"),
        P("area"),
        P("area"),
        P(("runs", "area"), None, None),
        P("area"),
        P("area"),
        P("area"),
        P(("runs", "area"), None, None),
    )
    return jax.shard_map(
        functools.partial(local, nz, ny), mesh=mesh, in_specs=placed, out_specs=P("runs", "area"), check_vma=False
    )
```

```python
import functools

import jax
import jax.numpy as jnp
from jax import lax
from jax.experimental import pallas as pl
from jax.experimental.pallas import tpu as pltpu
from jax.sharding import PartitionSpec as P

STEPS = 6
DMAX = 4
MOST_SEC = 6
SLICES = STEPS - 2 + DMAX
UNROLL = 16
MESH = pl.DeviceIdType.MESH


def kernel(nz, ny, *refs):
    remote_weight, local_weight = refs[9], refs[13]
    small = [*refs[:9], *refs[10:13]]
    out = refs[14]
    held_small = refs[15 : 15 + len(small)]
    (
        history, drive, leak, inhibition, section, link_source, link_block, link_target, link_delay,
        local_block, local_target, local_delay,
    ) = held_small
    rest = refs[15 + len(small) :]
    gathered = rest[:SLICES]
    own = rest[SLICES : SLICES + DMAX + STEPS - 1]
    (
        w_remote, w_local, sums, area_mask, place,
        in_sem, w_sem, sum_send, sum_recv, z_send, z_recv, y_send, y_recv, c_send, c_recv, d_send, d_recv,
    ) = rest[SLICES + DMAX + STEPS - 1 :]
    n = nz * ny * 2
    trials, width = drive.shape
    pop = w_remote.shape[1]
    blocks = width // pop
    links = link_block.shape[0]
    locals_ = local_block.shape[0]

    me = lax.axis_index("area")
    core = lax.rem(me, 2)
    y = lax.rem(me // 2, ny)
    z = me // (2 * ny)
    line = (y * 2 + core) * nz
    line_y = ((1 - y) * 2 + core) * nz
    my_place = line + z
    sibling = me + 1 - 2 * core
    across = me + (1 - 2 * y) * 2

    sums[...] = jnp.zeros_like(sums)

    barrier = pltpu.get_barrier_semaphore()

    @pl.loop(1, n)
    def _(k):
        pl.semaphore_signal(barrier, inc=1, device_id={"area": lax.rem(me + k, n)}, device_id_type=MESH)

    loads = [pltpu.make_async_copy(a, b, in_sem.at[i]) for i, (a, b) in enumerate(zip(small, held_small))]
    for load in loads:
        load.start()
    load_local = pltpu.make_async_copy(local_weight, w_local, w_sem.at[0])
    load_remote = pltpu.make_async_copy(remote_weight, w_remote, w_sem.at[1])
    load_local.start()
    load_remote.start()

    def keep(s, values):
        for b in range(blocks):
            own[s][b] = values[b]
            if s < SLICES:
                gathered[s][my_place * blocks + b] = values[b]

    loads[0].wait()
    for s in range(DMAX):
        keep(s, [history[DMAX - 1 - s, :, b * pop : (b + 1) * pop] for b in range(blocks)])

    rows = lax.broadcasted_iota(jnp.int32, (trials, 128), 0)
    lanes = lax.broadcasted_iota(jnp.int32, (trials, 128), 1)
    diagonal = rows == lanes

    def put_sum(t, values):
        total = values[0].astype(jnp.float32)
        for b in range(1, blocks):
            total = total + values[b].astype(jnp.float32)
        column = jnp.sum(total, axis=1, keepdims=True)
        row = jnp.sum(jnp.where(diagonal, column, 0.0), axis=0, keepdims=True)
        sums[t, pl.ds(me, 1), :] = row

    def each_mate(act):
        for i, k in enumerate(k for m in range(1, MOST_SEC) for k in (m, -m)):

            @pl.when((me + k >= 0) & (me + k < n))
            def _(i=i, k=k):
                act(i, k)

    def sum_copy(t, i, k):
        return pltpu.make_async_remote_copy(
            src_ref=sums.at[t, pl.ds(me, 1)],
            dst_ref=sums.at[t, pl.ds(me, 1)],
            send_sem=sum_send.at[t, i],
            recv_sem=sum_recv.at[t, i],
            device_id={"area": me + k},
            device_id_type=MESH,
        )

    def send_sums(t):
        each_mate(lambda i, k: sum_copy(t, i, k).start())

    def await_sums(t):
        each_mate(lambda i, k: await_bytes(sums.at[t, pl.ds(me + k, 1)], sum_recv.at[t, i ^ 1]))

    def await_bytes(ref, sem):
        pltpu.make_async_copy(ref, ref, sem).wait()

    def part(s, start, count):
        return gathered[s].at[pl.ds(start * blocks, count * blocks)]

    def xor(k):
        return sum((1 << b) * (1 - 2 * lax.rem(z // (1 << b), 2)) for b in range(2) if k >> b & 1) + z

    def each_other(act):
        if nz == 4:
            for k in range(1, nz):
                act(k, xor(k), xor(k))
        else:

            @pl.loop(1, nz)
            def _(k):
                act(k, lax.rem(z + k, nz), lax.rem(z + nz - k, nz))

    def copy(s, start, count, target, send, recv):
        return pltpu.make_async_remote_copy(
            src_ref=part(s, start, count),
            dst_ref=part(s, start, count),
            send_sem=send,
            recv_sem=recv,
            device_id={"area": target},
            device_id_type=MESH,
        )

    def y_copy(s, start):
        if ny == 2:
            copy(s, start, 1, across, y_send.at[s], y_recv.at[s]).start()

    def z_start(s):
        def send(k, to, source):
            copy(s, my_place, 1, (to * ny + y) * 2 + core, z_send.at[s], z_recv.at[s, k]).start()

        each_other(send)
        y_copy(s, my_place)

    def z_done(s):
        def forward(k, to, source):
            await_bytes(part(s, line + source, 1), z_recv.at[s, k])
            y_copy(s, line + source)

        each_other(forward)
        copy(s, line, nz, sibling, c_send.at[s], c_recv.at[s]).start()

    def y_done(s):
        if ny == 2:
            await_bytes(part(s, line_y, nz), y_recv.at[s])
            copy(s, line_y, nz, sibling, d_send.at[s], d_recv.at[s]).start()

    def c_done(s):
        await_bytes(part(s, line, nz), c_recv.at[s])
        if ny == 2:
            await_bytes(part(s, line_y, nz), d_recv.at[s])

    put_sum(0, [own[DMAX - 1][b] for b in range(blocks)])
    pl.semaphore_wait(barrier, n - 1)
    send_sums(0)
    for s in range(DMAX):
        z_start(s)

    for load in loads[1:]:
        load.wait()

    @pl.loop(0, links)
    def _(l):
        q = link_source[l]
        at = (lax.rem(q // 2, ny) * 2 + lax.rem(q, 2)) * nz + q // (2 * ny)
        place[l] = at * blocks + link_block[l]

    my_area = section[me]
    count = jnp.float32(0.0)
    for q in range(n):
        same = jnp.where(section[q] == my_area, 1.0, 0.0).astype(jnp.float32)
        count = count + same
        area_mask[q : q + 1, :] = jnp.full((1, 128), same, jnp.float32)
    inhibit = inhibition[my_area]
    neurons = jnp.full((1, 128), count * float(width), jnp.float32)

    zero = jnp.zeros((trials, pop), jnp.bfloat16)

    def dots(acc, total, sources, first, at_ref, delay_ref, target_ref, weight):
        def body(g, acc):
            columns = []
            for u in range(UNROLL):
                l = g * UNROLL + u
                at, delay, target = at_ref[l], delay_ref[l], target_ref[l]
                x = sources[-1][at]
                for i in range(len(sources) - 2, -1, -1):
                    x = lax.select(delay == first + i, sources[i][at], x)
                columns.append(jnp.concatenate([lax.select(target == b, x, zero) for b in range(blocks)], axis=0))
            lhs = jnp.concatenate(columns, axis=1)
            w = weight[pl.ds(g * UNROLL, UNROLL)].reshape(UNROLL * pop, pop)
            return acc + jnp.dot(lhs, w, preferred_element_type=jnp.float32)

        return lax.fori_loop(0, total // UNROLL, body, acc)

    def local_dots(t, acc):
        return dots(
            acc, locals_, [own[t + DMAX - d] for d in range(1, DMAX + 1)], 1, local_block, local_delay, local_target, w_local
        )

    def remote_dots(t, acc):
        return dots(
            acc, links, [gathered[t + DMAX - d] for d in range(2, DMAX + 1)], 2, place, link_delay, link_target, w_remote
        )

    def finish(t, acc):
        await_sums(t)
        total = jnp.sum(sums[t] * area_mask[...], axis=0, keepdims=True)
        row = inhibit * (total / neurons)
        held = jnp.sum(jnp.where(diagonal, row, 0.0), axis=1, keepdims=True)
        fresh = []
        for b in range(blocks):
            cut = slice(b * pop, (b + 1) * pop)
            gain = leak[:, cut]
            pushed = acc[b * trials : (b + 1) * trials] + drive[:, cut].astype(jnp.float32) - held
            previous = own[t + DMAX - 1][b].astype(jnp.float32)
            fresh.append(((1.0 - gain) * previous + gain * jax.nn.sigmoid(pushed)).astype(jnp.bfloat16))
        return fresh

    for t in range(STEPS):
        acc = jnp.zeros((blocks * trials, pop), jnp.float32)
        if t == 0:
            load_local.wait()
            acc = local_dots(t, acc)
            z_done(0)
            z_done(1)
            y_done(0)
            z_done(2)
            y_done(1)
            z_done(3)
            y_done(2)
            load_remote.wait()
            for s in range(DMAX - 1):
                c_done(s)
            acc = remote_dots(t, acc)
            y_done(3)
        else:
            acc = local_dots(t, acc)
            if t >= 2:
                y_done(t + DMAX - 2)
            c_done(t + DMAX - 2)
            if t + DMAX - 1 < SLICES:
                z_done(t + DMAX - 1)
            acc = remote_dots(t, acc)
        fresh = finish(t, acc)
        if t == STEPS - 1:
            for b in range(blocks):
                out[:, b * pop : (b + 1) * pop] = fresh[b]
        else:
            keep(t + DMAX, fresh)
            put_sum(t + 1, fresh)
            send_sums(t + 1)
            if t + DMAX < SLICES:
                z_start(t + DMAX)

    for t in range(STEPS):
        each_mate(lambda i, k: sum_copy(t, i, k).wait_send())
    for s in range(SLICES):
        await_bytes(part(s, line, nz - 1), z_send.at[s])
        await_bytes(part(s, line, nz), c_send.at[s])
        if ny == 2:
            await_bytes(part(s, line, nz), y_send.at[s])
            await_bytes(part(s, line_y, nz), d_send.at[s])


def local(nz, ny, *args):
    (history, drive, leak, inhibition, section, link_source, *others) = args
    remote_weight, local_weight = others[3], others[7]
    depth, trials, width = history.shape
    pop = remote_weight.shape[1]
    blocks = width // pop
    n = nz * ny * 2
    operands = [history, drive, leak.reshape(1, -1), inhibition, section, link_source.reshape(-1), *others]
    small = [*operands[:9], *operands[10:13]]
    dma = pltpu.SemaphoreType.DMA
    return pl.pallas_call(
        functools.partial(kernel, nz, ny),
        out_shape=jax.ShapeDtypeStruct((trials, width), jnp.bfloat16),
        in_specs=[pl.BlockSpec(memory_space=pltpu.HBM)] * len(operands),
        out_specs=pl.BlockSpec(memory_space=pltpu.VMEM),
        scratch_shapes=[
            *[pltpu.VMEM(a.shape, a.dtype) for a in small[:3]],
            *[pltpu.SMEM(a.shape, a.dtype) for a in small[3:]],
            *[pltpu.VMEM((n * blocks, trials, pop), jnp.bfloat16) for _ in range(SLICES)],
            *[pltpu.VMEM((blocks, trials, pop), jnp.bfloat16) for _ in range(DMAX + STEPS - 1)],
            pltpu.VMEM(remote_weight.shape, jnp.bfloat16),
            pltpu.VMEM(local_weight.shape, jnp.bfloat16),
            pltpu.VMEM((STEPS, n, 128), jnp.float32),
            pltpu.VMEM((n, 128), jnp.float32),
            pltpu.SMEM((link_source.shape[0],), jnp.int32),
            dma((len(small),)),
            dma((2,)),
            dma((STEPS, 2 * (MOST_SEC - 1))),
            dma((STEPS, 2 * (MOST_SEC - 1))),
            dma((SLICES,)),
            dma((SLICES, nz)),
            *[dma((SLICES,)) for _ in range(6)],
        ],
        compiler_params=pltpu.CompilerParams(
            collective_id=0, has_side_effects=True, vmem_limit_bytes=60 * 1024 * 1024
        ),
    )(*operands)


def solution(mesh):
    ny = 2 if mesh.shape["runs"] == 2 else 1
    nz = mesh.shape["area"] // (2 * ny)
    placed = (
        P(None, "runs", "area"),
        P("runs", "area"),
        P(("runs", "area")),
        P("runs"),
        P(),
        P("area", None),
        P("area"),
        P("area"),
        P("area"),
        P(("runs", "area"), None, None),
        P("area"),
        P("area"),
        P("area"),
        P(("runs", "area"), None, None),
    )
    return jax.shard_map(
        functools.partial(local, nz, ny), mesh=mesh, in_specs=placed, out_specs=P("runs", "area"), check_vma=False
    )
```

```python
import functools

import jax
import jax.numpy as jnp
from jax import lax
from jax.experimental import pallas as pl
from jax.experimental.pallas import tpu as pltpu
from jax.sharding import PartitionSpec as P

STEPS = 6
DMAX = 4
MOST_SEC = 6
SLICES = STEPS - 2 + DMAX
UNROLL = 16
MESH = pl.DeviceIdType.MESH


def kernel(nz, ny, *refs):
    remote_weight, local_weight = refs[9], refs[13]
    small = [*refs[:9], *refs[10:13]]
    out = refs[14]
    held_small = refs[15 : 15 + len(small)]
    (
        history, drive, leak, inhibition, section, link_source, link_block, link_target, link_delay,
        local_block, local_target, local_delay,
    ) = held_small
    rest = refs[15 + len(small) :]
    gathered = rest[:SLICES]
    own = rest[SLICES : SLICES + DMAX + STEPS - 1]
    (
        w_remote, w_local, sums, area_mask, place,
        in_sem, w_sem, sum_send, sum_recv, z_send, z_recv, y_send, y_recv, c_send, c_recv, d_send, d_recv,
    ) = rest[SLICES + DMAX + STEPS - 1 :]
    n = nz * ny * 2
    trials, width = drive.shape
    pop = w_remote.shape[1]
    blocks = width // pop
    links = link_block.shape[0]
    locals_ = local_block.shape[0]

    me = lax.axis_index("area")
    core = lax.rem(me, 2)
    y = lax.rem(me // 2, ny)
    z = me // (2 * ny)
    line = (y * 2 + core) * nz
    line_y = ((1 - y) * 2 + core) * nz
    my_place = line + z
    sibling = me + 1 - 2 * core
    across = me + (1 - 2 * y) * 2

    sums[...] = jnp.zeros_like(sums)

    barrier = pltpu.get_barrier_semaphore()

    @pl.loop(1, n)
    def _(k):
        pl.semaphore_signal(barrier, inc=1, device_id={"area": lax.rem(me + k, n)}, device_id_type=MESH)

    loads = [pltpu.make_async_copy(a, b, in_sem.at[i]) for i, (a, b) in enumerate(zip(small, held_small))]
    for load in loads:
        load.start()
    load_local = pltpu.make_async_copy(local_weight, w_local, w_sem.at[0])
    load_remote = pltpu.make_async_copy(remote_weight, w_remote, w_sem.at[1])
    load_local.start()
    load_remote.start()

    def keep(s, values):
        for b in range(blocks):
            own[s][b] = values[b]
            if s < SLICES:
                gathered[s][my_place * blocks + b] = values[b]

    loads[0].wait()
    for s in range(DMAX):
        keep(s, [history[DMAX - 1 - s, :, b * pop : (b + 1) * pop] for b in range(blocks)])

    rows = lax.broadcasted_iota(jnp.int32, (trials, 128), 0)
    lanes = lax.broadcasted_iota(jnp.int32, (trials, 128), 1)
    diagonal = rows == lanes

    def put_sum(t, values):
        total = values[0].astype(jnp.float32)
        for b in range(1, blocks):
            total = total + values[b].astype(jnp.float32)
        column = jnp.sum(total, axis=1, keepdims=True)
        row = jnp.sum(jnp.where(diagonal, column, 0.0), axis=0, keepdims=True)
        sums[t, pl.ds(me, 1), :] = row

    def each_mate(act):
        for i, k in enumerate(k for m in range(1, MOST_SEC) for k in (m, -m)):

            @pl.when((me + k >= 0) & (me + k < n))
            def _(i=i, k=k):
                act(i, k)

    def sum_copy(t, i, k):
        return pltpu.make_async_remote_copy(
            src_ref=sums.at[t, pl.ds(me, 1)],
            dst_ref=sums.at[t, pl.ds(me, 1)],
            send_sem=sum_send.at[t, i],
            recv_sem=sum_recv.at[t, i],
            device_id={"area": me + k},
            device_id_type=MESH,
        )

    def send_sums(t):
        each_mate(lambda i, k: sum_copy(t, i, k).start())

    def await_sums(t):
        each_mate(lambda i, k: await_bytes(sums.at[t, pl.ds(me + k, 1)], sum_recv.at[t, i ^ 1]))

    def await_bytes(ref, sem):
        pltpu.make_async_copy(ref, ref, sem).wait()

    def part(s, start, count):
        return gathered[s].at[pl.ds(start * blocks, count * blocks)]

    def xor(k):
        return sum((1 << b) * (1 - 2 * lax.rem(z // (1 << b), 2)) for b in range(2) if k >> b & 1) + z

    def each_other(act):
        if nz == 4:
            for k in range(1, nz):
                act(k, xor(k), xor(k))
        else:

            @pl.loop(1, nz)
            def _(k):
                act(k, lax.rem(z + k, nz), lax.rem(z + nz - k, nz))

    def copy(s, start, count, target, send, recv):
        return pltpu.make_async_remote_copy(
            src_ref=part(s, start, count),
            dst_ref=part(s, start, count),
            send_sem=send,
            recv_sem=recv,
            device_id={"area": target},
            device_id_type=MESH,
        )

    def y_copy(s, start):
        if ny == 2:
            copy(s, start, 1, across, y_send.at[s], y_recv.at[s]).start()

    def z_start(s):
        def send(k, to, source):
            copy(s, my_place, 1, (to * ny + y) * 2 + core, z_send.at[s], z_recv.at[s, k]).start()

        each_other(send)
        y_copy(s, my_place)

    def z_done(s):
        def forward(k, to, source):
            await_bytes(part(s, line + source, 1), z_recv.at[s, k])
            y_copy(s, line + source)

        each_other(forward)
        copy(s, line, nz, sibling, c_send.at[s], c_recv.at[s]).start()

    def y_done(s):
        if ny == 2:
            await_bytes(part(s, line_y, nz), y_recv.at[s])
            copy(s, line_y, nz, sibling, d_send.at[s], d_recv.at[s]).start()

    def c_done(s):
        await_bytes(part(s, line, nz), c_recv.at[s])
        if ny == 2:
            await_bytes(part(s, line_y, nz), d_recv.at[s])

    put_sum(0, [own[DMAX - 1][b] for b in range(blocks)])
    pl.semaphore_wait(barrier, n - 1)
    send_sums(0)
    for s in range(DMAX):
        z_start(s)

    for load in loads[1:]:
        load.wait()

    @pl.loop(0, links)
    def _(l):
        q = link_source[l]
        at = (lax.rem(q // 2, ny) * 2 + lax.rem(q, 2)) * nz + q // (2 * ny)
        place[l] = at * blocks + link_block[l]

    my_area = section[me]
    count = jnp.float32(0.0)
    for q in range(n):
        same = jnp.where(section[q] == my_area, 1.0, 0.0).astype(jnp.float32)
        count = count + same
        area_mask[q : q + 1, :] = jnp.full((1, 128), same, jnp.float32)
    inhibit = inhibition[my_area]
    neurons = jnp.full((1, 128), count * float(width), jnp.float32)

    zero = jnp.zeros((trials, pop), jnp.bfloat16)

    def dots(acc, total, sources, first, at_ref, delay_ref, target_ref, weight):
        def body(g, acc):
            columns = []
            for u in range(UNROLL):
                l = g * UNROLL + u
                at, delay, target = at_ref[l], delay_ref[l], target_ref[l]
                x = sources[-1][at]
                for i in range(len(sources) - 2, -1, -1):
                    x = lax.select(delay == first + i, sources[i][at], x)
                columns.append(jnp.concatenate([lax.select(target == b, x, zero) for b in range(blocks)], axis=0))
            lhs = jnp.concatenate(columns, axis=1)
            w = weight[pl.ds(g * UNROLL, UNROLL)].reshape(UNROLL * pop, pop)
            return acc + jnp.dot(lhs, w, preferred_element_type=jnp.float32)

        return lax.fori_loop(0, total // UNROLL, body, acc)

    def local_dots(t, acc):
        return dots(
            acc, locals_, [own[t + DMAX - d] for d in range(1, DMAX + 1)], 1, local_block, local_delay, local_target, w_local
        )

    def remote_dots(t, acc):
        return dots(
            acc, links, [gathered[t + DMAX - d] for d in range(2, DMAX + 1)], 2, place, link_delay, link_target, w_remote
        )

    def finish(t, acc):
        await_sums(t)
        total = jnp.sum(sums[t] * area_mask[...], axis=0, keepdims=True)
        row = inhibit * (total / neurons)
        held = jnp.sum(jnp.where(diagonal, row, 0.0), axis=1, keepdims=True)
        fresh = []
        for b in range(blocks):
            cut = slice(b * pop, (b + 1) * pop)
            gain = leak[:, cut]
            pushed = acc[b * trials : (b + 1) * trials] + drive[:, cut].astype(jnp.float32) - held
            previous = own[t + DMAX - 1][b].astype(jnp.float32)
            fresh.append(((1.0 - gain) * previous + gain * jax.nn.sigmoid(pushed)).astype(jnp.bfloat16))
        return fresh

    for t in range(STEPS):
        acc = jnp.zeros((blocks * trials, pop), jnp.float32)
        if t == 0:
            load_local.wait()
            acc = local_dots(t, acc)
            z_done(0)
            z_done(1)
            y_done(0)
            z_done(2)
            y_done(1)
            y_done(2)
            load_remote.wait()
            for s in range(DMAX - 1):
                c_done(s)
            acc = remote_dots(t, acc)
            z_done(3)
        else:
            acc = local_dots(t, acc)
            y_done(t + DMAX - 2)
            c_done(t + DMAX - 2)
            if t + DMAX - 1 < SLICES:
                z_done(t + DMAX - 1)
            acc = remote_dots(t, acc)
        fresh = finish(t, acc)
        if t == STEPS - 1:
            for b in range(blocks):
                out[:, b * pop : (b + 1) * pop] = fresh[b]
        else:
            keep(t + DMAX, fresh)
            put_sum(t + 1, fresh)
            send_sums(t + 1)
            if t + DMAX < SLICES:
                z_start(t + DMAX)

    for t in range(STEPS):
        each_mate(lambda i, k: sum_copy(t, i, k).wait_send())
    for s in range(SLICES):
        await_bytes(part(s, line, nz - 1), z_send.at[s])
        await_bytes(part(s, line, nz), c_send.at[s])
        if ny == 2:
            await_bytes(part(s, line, nz), y_send.at[s])
            await_bytes(part(s, line_y, nz), d_send.at[s])


def local(nz, ny, *args):
    (history, drive, leak, inhibition, section, link_source, *others) = args
    remote_weight, local_weight = others[3], others[7]
    depth, trials, width = history.shape
    pop = remote_weight.shape[1]
    blocks = width // pop
    n = nz * ny * 2
    operands = [history, drive, leak.reshape(1, -1), inhibition, section, link_source.reshape(-1), *others]
    small = [*operands[:9], *operands[10:13]]
    dma = pltpu.SemaphoreType.DMA
    return pl.pallas_call(
        functools.partial(kernel, nz, ny),
        out_shape=jax.ShapeDtypeStruct((trials, width), jnp.bfloat16),
        in_specs=[pl.BlockSpec(memory_space=pltpu.HBM)] * len(operands),
        out_specs=pl.BlockSpec(memory_space=pltpu.VMEM),
        scratch_shapes=[
            *[pltpu.VMEM(a.shape, a.dtype) for a in small[:3]],
            *[pltpu.SMEM(a.shape, a.dtype) for a in small[3:]],
            *[pltpu.VMEM((n * blocks, trials, pop), jnp.bfloat16) for _ in range(SLICES)],
            *[pltpu.VMEM((blocks, trials, pop), jnp.bfloat16) for _ in range(DMAX + STEPS - 1)],
            pltpu.VMEM(remote_weight.shape, jnp.bfloat16),
            pltpu.VMEM(local_weight.shape, jnp.bfloat16),
            pltpu.VMEM((STEPS, n, 128), jnp.float32),
            pltpu.VMEM((n, 128), jnp.float32),
            pltpu.SMEM((link_source.shape[0],), jnp.int32),
            dma((len(small),)),
            dma((2,)),
            dma((STEPS, 2 * (MOST_SEC - 1))),
            dma((STEPS, 2 * (MOST_SEC - 1))),
            dma((SLICES,)),
            dma((SLICES, nz)),
            *[dma((SLICES,)) for _ in range(6)],
        ],
        compiler_params=pltpu.CompilerParams(
            collective_id=0, has_side_effects=True, vmem_limit_bytes=60 * 1024 * 1024
        ),
    )(*operands)


def solution(mesh):
    ny = 2 if mesh.shape["runs"] == 2 else 1
    nz = mesh.shape["area"] // (2 * ny)
    placed = (
        P(None, "runs", "area"),
        P("runs", "area"),
        P(("runs", "area")),
        P("runs"),
        P(),
        P("area", None),
        P("area"),
        P("area"),
        P("area"),
        P(("runs", "area"), None, None),
        P("area"),
        P("area"),
        P("area"),
        P(("runs", "area"), None, None),
    )
    return jax.shard_map(
        functools.partial(local, nz, ny), mesh=mesh, in_specs=placed, out_specs=P("runs", "area"), check_vma=False
    )
```
